32 devices in a mesh: blk: 8 (over z, x), heads: 4 (over y, core).
Axes of the slice: x: 2, y: 2, z: 4, core: 2. Of those that a mesh axis runs over, the one named last changes fastest.
Arguments:
- queries: float32 [512, 8192], P('blk', 'heads'), may hold values from -6 to 6
- visual_keys: float32 [8192, 1024], P('blk', 'heads'), may hold values from -6 to 6
- projected_values: float32 [8192, 1024], P('blk', 'heads'), may hold values from -6 to 6
- valid_lengths: int32 [8], P('blk'), may hold values from 256 to 1024, as said below
Outputs:
- attended: float32 [512, 8192], P('blk', 'heads')
The draws below stay inside these ranges and needn't reach their ends.
Inputs may be any that keep to these rules, and one draw needn't show every extreme that they name: `valid_lengths`: some block has all 1024 tokens valid in every draw.
All inputs are finite; a program needn't handle non-finite values.
Results may differ from the reference program's by a relative error of at most 0.0003.
Values sent between devices are 32-bit elements; how exact they have to be, the bound alone decides.
A program may use at most 64 MiB of HBM per device.

```python
import jax
import jax.numpy as jnp
from jax import lax

QH = 64
KEY_VALUE_HEADS = 8
HEAD_DIM = 128
QB = 64
BLOCK_TOKENS = 1024
WIN = 4
NQ = 512
TOTAL_TOKENS = 8192


def draw_queries(key, part):
    local_key = jax.random.fold_in(key, 3)
    return jnp.clip(1.6 * jax.random.normal(local_key, (NQ, QH * HEAD_DIM), jnp.float32), -6.0, 6.0)


def draw_visual_keys(key, part):
    local_key = jax.random.fold_in(key, 7)
    return jnp.clip(1.6 * jax.random.normal(local_key, (TOTAL_TOKENS, KEY_VALUE_HEADS * HEAD_DIM), jnp.float32), -6.0, 6.0)


def draw_valid_lengths(key, part):
    shard_blocks = TOTAL_TOKENS // BLOCK_TOKENS
    picks = jax.random.randint(jax.random.fold_in(key, 23), (shard_blocks,), BLOCK_TOKENS // 4, BLOCK_TOKENS + 1)
    chosen = jax.random.randint(jax.random.fold_in(key, 29), (), 0, shard_blocks)
    return jnp.where(jnp.arange(shard_blocks) == chosen, BLOCK_TOKENS, picks).astype(jnp.int32)


def shard_levels(key, dims, split, least, top_value):
    def one(axis_at, shards_of):
        steps = jax.random.uniform(jax.random.fold_in(jax.random.fold_in(key, 6), axis_at), (shards_of,), jnp.float32, least / len(split), top_value / len(split))
        return jnp.repeat(jnp.exp(steps), dims[axis_at] // shards_of).reshape((-1,) + (1,) * (len(dims) - axis_at - 1))

    gain = one(*split[0])
    for cut in split[1:]:
        gain = gain * one(*cut)
    return gain


def scatter_about(stream_key, extent, scale, limit, pieces=(), kind=jnp.bfloat16):
    drawn = scale * jax.random.normal(stream_key, extent, jnp.float32)
    if pieces:
        drawn = drawn * shard_levels(stream_key, extent, pieces, -0.22, 0.18)
    return jnp.clip(drawn, -limit, limit).astype(kind)


def setup_inputs(seed: int = 0) -> dict:
    key_list = jax.random.split(jax.random.key(seed), 5)
    queries = draw_queries(jax.random.fold_in(key_list[4], 71), 0)
    visual_keys = draw_visual_keys(jax.random.fold_in(key_list[4], 71), 0)
    projected_values = scatter_about(key_list[2], (TOTAL_TOKENS, KEY_VALUE_HEADS * HEAD_DIM), 1.0, 6.0, ((0, 8), (1, 4)), jnp.float32)
    valid_lengths = draw_valid_lengths(jax.random.fold_in(key_list[4], 71), 0)
    return {"queries": queries, "visual_keys": visual_keys, "projected_values": projected_values, "valid_lengths": valid_lengths}


def reference(queries, visual_keys, projected_values, valid_lengths):
    shard_blocks = TOTAL_TOKENS // BLOCK_TOKENS
    left_reach = WIN // 2 - 1
    right_reach = WIN // 2
    group_size = QH // KEY_VALUE_HEADS
    scaled = queries * (HEAD_DIM ** -0.5)
    key_blocks = jnp.pad(visual_keys.reshape(shard_blocks, BLOCK_TOKENS, KEY_VALUE_HEADS, HEAD_DIM), ((left_reach, right_reach), (0, 0), (0, 0), (0, 0)))
    value_blocks = jnp.pad(projected_values.reshape(shard_blocks, BLOCK_TOKENS, KEY_VALUE_HEADS, HEAD_DIM), ((left_reach, right_reach), (0, 0), (0, 0), (0, 0)))
    counts = jnp.pad(valid_lengths, (left_reach, right_reach))
    positions = jnp.arange(BLOCK_TOKENS, dtype=jnp.int32)

    def one_block(block_index):
        query_tile = lax.dynamic_slice_in_dim(scaled, block_index * QB, QB, 0).reshape(QB, KEY_VALUE_HEADS, group_size, HEAD_DIM)
        window_keys = lax.dynamic_slice_in_dim(key_blocks, block_index, WIN, 0).reshape(WIN * BLOCK_TOKENS, KEY_VALUE_HEADS, HEAD_DIM)
        window_values = lax.dynamic_slice_in_dim(value_blocks, block_index, WIN, 0).reshape(WIN * BLOCK_TOKENS, KEY_VALUE_HEADS, HEAD_DIM)
        window_counts = lax.dynamic_slice_in_dim(counts, block_index, WIN, 0)
        usable = (positions[None, :] < window_counts[:, None]).reshape(WIN * BLOCK_TOKENS)
        scores = jnp.einsum("qhgd,khd->hgqk", query_tile, window_keys, precision=lax.Precision.HIGHEST)
        scores = jnp.where(usable, scores, -jnp.inf)
        peak_score = jnp.max(scores, axis=-1, keepdims=True)
        weights = jnp.exp(scores - peak_score)
        weight_sum = jnp.sum(weights, axis=-1)
        numerator = jnp.einsum("hgqk,khd->qhgd", weights, window_values, precision=lax.Precision.HIGHEST)
        return (numerator / jnp.transpose(weight_sum, (2, 0, 1))[..., None]).reshape(QB, QH * HEAD_DIM)

    blocks = lax.map(one_block, jnp.arange(shard_blocks, dtype=jnp.int32))
    return blocks.reshape(NQ, QH * HEAD_DIM)
```

```python
import functools
import math

import jax
import jax.numpy as jnp
from jax import lax
from jax.experimental import pallas as pl
from jax.experimental.pallas import tpu as pltpu
from jax.sharding import PartitionSpec as P

HEAD_DIM = 128
SPAN = 6
CH = 4
MESH = pl.DeviceIdType.MESH
F32 = jnp.float32
BF16 = jnp.bfloat16


def split2(a):
    hi = a.astype(BF16)
    return hi, (a - hi.astype(F32)).astype(BF16)


def pair_kernel(
    blocks, group, n_ref, q_hbm, k_hbm, v_hbm, out_ref,
    kraw, vraw, ka, kb, va, q_own, qx, qz, qf,
    own_num, own_st, loc_num, loc_st,
    px_s, pz_s, pf_s, px_r, pz_r, pf_r,
    lsem, q_ss, q_rs, p_ss, p_rs,
):
    b = lax.axis_index("blk")
    x = lax.rem(b, 2)
    rows = q_own.shape[0]
    keys = kraw.shape[0]
    kv = kraw.shape[1] // HEAD_DIM
    chunks = q_own.shape[1] // (CH * HEAD_DIM)
    tb = rows // 8
    partner = b + 1 - 2 * x
    up, down = b + 2, b - 2
    has_up, has_down = up < blocks, down >= 0
    fdst, fsrc = b + 2 - 4 * x, b - 2 + 4 * x
    has_fdst = (fdst >= 0) & (fdst < blocks)
    has_fsrc = (fsrc >= 0) & (fsrc < blocks)

    barrier = pltpu.get_barrier_semaphore()
    pl.semaphore_signal(barrier, inc=1, device_id={"blk": partner}, device_id_type=MESH)

    @pl.when(has_up)
    def _():
        pl.semaphore_signal(barrier, inc=1, device_id={"blk": up}, device_id_type=MESH)

    @pl.when(has_down)
    def _():
        pl.semaphore_signal(barrier, inc=1, device_id={"blk": down}, device_id_type=MESH)

    own_copy = pltpu.make_async_copy(q_hbm, q_own, lsem.at[0])
    k_copy = pltpu.make_async_copy(k_hbm, kraw, lsem.at[1])
    v_copy = pltpu.make_async_copy(v_hbm, vraw, lsem.at[2])
    k_copy.start()
    v_copy.start()
    own_copy.start()
    pl.semaphore_wait(
        barrier, 1 + jnp.where(has_up, 1, 0) + jnp.where(has_down, 1, 0)
    )

    def cols(c):
        return pl.ds(pl.multiple_of(c * (CH * HEAD_DIM), CH * HEAD_DIM), CH * HEAD_DIM)

    def qcopy(kind, src, dst, c, to):
        return pltpu.make_async_remote_copy(
            src_ref=src.at[:, cols(c)], dst_ref=dst.at[:, cols(c)],
            send_sem=q_ss.at[kind, c], recv_sem=q_rs.at[kind, c],
            device_id={"blk": to}, device_id_type=MESH,
        )

    def x_copy(c):
        return qcopy(0, q_hbm, qx, c, partner)

    def z_copy(c):
        return qcopy(1, q_hbm, qz, c, up)

    def f_copy(c):
        return qcopy(2, qx, qf, c, fdst)

    def pcopy(kind, src, dst, c, to):
        return pltpu.make_async_remote_copy(
            src_ref=src.at[c], dst_ref=dst.at[c],
            send_sem=p_ss.at[kind, c], recv_sem=p_rs.at[kind, c],
            device_id={"blk": to}, device_id_type=MESH,
        )

    def px_copy(c):
        return pcopy(0, px_s, px_r, c, partner)

    def pz_copy(c):
        return pcopy(1, pz_s, pz_r, c, down)

    def pf_copy(c):
        return pcopy(2, pf_s, pf_r, c, fsrc)

    def start_x(c, carry):
        x_copy(c).start()
        return carry

    lax.fori_loop(0, chunks, start_x, 0)

    @pl.when(has_up)
    def _():
        z_copy(0).start()

    lane = lax.broadcasted_iota(jnp.int32, (rows, HEAD_DIM), 1)
    valid = n_ref[0]
    klane = lax.broadcasted_iota(jnp.int32, (keys, HEAD_DIM), 1)
    krow = lax.broadcasted_iota(jnp.int32, (keys, HEAD_DIM), 0)
    bias = jnp.where((klane == 0) & (krow >= valid), -1e30, 0.0).astype(BF16)
    k_copy.wait()
    for g in range(kv):
        hi, lo = split2(kraw[:, g * HEAD_DIM:(g + 1) * HEAD_DIM])
        ka[g, :, :HEAD_DIM] = hi
        ka[g, :, HEAD_DIM:] = hi
        kb[g, :, :HEAD_DIM] = lo
        kb[g, :, HEAD_DIM:] = bias
    v_copy.wait()
    for g in range(kv):
        hi, lo = split2(vraw[:, g * HEAD_DIM:(g + 1) * HEAD_DIM])
        va[g, :, :HEAD_DIM] = hi
        va[g, :, HEAD_DIM:] = lo
    own_copy.wait()

    qlane = lax.broadcasted_iota(jnp.int32, (CH * rows, HEAD_DIM), 1)
    one = jnp.where(qlane == 0, 1.0, 0.0).astype(BF16)
    scale = HEAD_DIM ** (-0.5) * math.log2(math.e)

    def attend(q_ref, c):
        g = (c * CH) // group
        q = q_ref[:, cols(c)]
        q = jnp.concatenate(
            [q[:, h * HEAD_DIM:(h + 1) * HEAD_DIM] for h in range(CH)], axis=0
        ) * scale
        hi, lo = split2(q)
        dims = (((1,), (1,)), ((), ()))
        s = lax.dot_general(
            jnp.concatenate([hi, lo], axis=1), ka[g], dims, preferred_element_type=F32
        ) + lax.dot_general(
            jnp.concatenate([hi, one], axis=1), kb[g], dims, preferred_element_type=F32
        )
        m = jnp.max(s, axis=1, keepdims=True)
        p = jnp.exp2(s - m)
        l = jnp.sum(p, axis=1, keepdims=True)
        p_hi, p_lo = split2(p)
        r = jnp.dot(p_hi, va[g], preferred_element_type=F32)
        num = r[:, :HEAD_DIM] + r[:, HEAD_DIM:] + jnp.dot(
            p_lo, va[g, :, :HEAD_DIM], preferred_element_type=F32
        )
        st = jnp.zeros((rows, HEAD_DIM), F32)
        for h in range(CH):
            st = jnp.where(lane == h, m[h * rows:(h + 1) * rows], st)
            st = jnp.where(lane == CH + h, l[h * rows:(h + 1) * rows], st)
        return num, st

    def pack(buf, c, num, st):
        buf[c, :CH * tb] = num.reshape(CH * tb, 8, HEAD_DIM)
        wide = jnp.concatenate([st] * (HEAD_DIM // rows), axis=0)
        buf[c, CH * tb] = wide.T[:8]

    def unpack(buf, c):
        num = buf[c, :CH * tb].reshape(CH * rows, HEAD_DIM)
        st = jnp.concatenate([buf[c, CH * tb]] * (HEAD_DIM // 8), axis=0).T[:rows]
        return num, st

    def column(st, h):
        return st[:, h:h + 1]

    def merge(a, o):
        top = jnp.maximum(a[1], o[1])
        fa, fo = jnp.exp2(a[1] - top), jnp.exp2(o[1] - top)
        total = a[1] * pltpu.roll(fa, CH, 1) + o[1] * pltpu.roll(fo, CH, 1)
        st = jnp.where(lane < CH, top, total)
        parts = []
        for h in range(CH):
            part = slice(h * rows, (h + 1) * rows)
            parts.append(a[0][part] * column(fa, h) + o[0][part] * column(fo, h))
        return jnp.concatenate(parts, axis=0), st

    def step(t, carry):
        early = t < chunks
        zc = jnp.where(t == 0, 0, t - chunks)
        late = (t == 0) | ((t > chunks) & (zc < chunks))

        @pl.when(late)
        def _():
            num, st = attend(q_own, zc)
            own_num[zc] = num
            own_st[zc] = st

        @pl.when(early)
        def _():
            x_copy(t).wait_recv()

            @pl.when(has_fdst)
            def _():
                f_copy(t).start()

            num, st = attend(qx, t)
            loc_num[t] = num
            loc_st[t] = st

        @pl.when((t == chunks - 1) & has_up)
        def _():
            def start_z(c, carry):
                z_copy(c).start()
                return carry

            lax.fori_loop(1, chunks, start_z, 0)

        @pl.when(late & has_down)
        def _():
            z_copy(zc).wait_recv()
            num, st = attend(qz, zc)
            pack(pz_s, zc, num, st)
            pz_copy(zc).start()

        fc = t - 1

        @pl.when((fc >= 0) & (fc < chunks) & has_fsrc)
        def _():
            f_copy(fc).wait_recv()
            num, st = attend(qf, fc)
            pack(pf_s, fc, num, st)
            pf_copy(fc).start()

        mc = t - 2

        @pl.when((mc >= 0) & (mc < chunks))
        def _():
            @pl.when(has_fdst)
            def _():
                pf_copy(mc).wait_recv()
                num, st = merge((loc_num[mc], loc_st[mc]), unpack(pf_r, mc))
                pack(px_s, mc, num, st)

            @pl.when(jnp.logical_not(has_fdst))
            def _():
                pack(px_s, mc, loc_num[mc], loc_st[mc])

            px_copy(mc).start()

        return carry

    lax.fori_loop(0, 2 * chunks, step, 0)

    def finish(c, carry):
        px_copy(c).wait_recv()
        num, st = merge((own_num[c], own_st[c]), unpack(px_r, c))
        own_num[c] = num
        own_st[c] = st

        @pl.when(has_up)
        def _():
            pz_copy(c).wait_recv()
            num, st = merge((own_num[c], own_st[c]), unpack(pz_r, c))
            own_num[c] = num
            own_st[c] = st

        st = own_st[c]
        num = own_num[c]
        out_ref[:, cols(c)] = jnp.concatenate(
            [num[h * rows:(h + 1) * rows] / column(st, CH + h) for h in range(CH)], axis=1
        )
        return carry

    lax.fori_loop(0, chunks, finish, 0)

    def drain(c, carry):
        x_copy(c).wait_send()
        px_copy(c).wait_send()

        @pl.when(has_up)
        def _():
            z_copy(c).wait_send()

        @pl.when(has_down)
        def _():
            pz_copy(c).wait_send()

        @pl.when(has_fdst)
        def _():
            f_copy(c).wait_send()

        @pl.when(has_fsrc)
        def _():
            pf_copy(c).wait_send()

        return carry

    lax.fori_loop(0, chunks, drain, 0)


def paired(queries, visual_keys, projected_values, valid_lengths):
    blocks = lax.axis_size("blk")
    rows, width = queries.shape
    keys, kv_width = visual_keys.shape
    kv = kv_width // HEAD_DIM
    group = width // kv_width
    chunks = width // (CH * HEAD_DIM)
    tiles = CH * rows // 8 + 1
    vmem = pltpu.VMEM
    part = vmem((chunks, tiles, 8, HEAD_DIM), F32)
    any_spec = pl.BlockSpec(memory_space=pl.ANY)
    pairs = 4 * rows * (width // HEAD_DIM) * keys
    return pl.pallas_call(
        functools.partial(pair_kernel, blocks, group),
        out_shape=jax.ShapeDtypeStruct((rows, width), F32),
        in_specs=[pl.BlockSpec(memory_space=pltpu.SMEM), any_spec, any_spec, any_spec],
        out_specs=pl.BlockSpec(memory_space=vmem),
        scratch_shapes=[
            vmem((keys, kv_width), F32),
            vmem((keys, kv_width), F32),
            vmem((kv, keys, 2 * HEAD_DIM), BF16),
            vmem((kv, keys, 2 * HEAD_DIM), BF16),
            vmem((kv, keys, 2 * HEAD_DIM), BF16),
            vmem((rows, width), F32),
            vmem((rows, width), F32),
            vmem((rows, width), F32),
            vmem((rows, width), F32),
            vmem((chunks, CH * rows, HEAD_DIM), F32),
            vmem((chunks, rows, HEAD_DIM), F32),
            vmem((chunks, CH * rows, HEAD_DIM), F32),
            vmem((chunks, rows, HEAD_DIM), F32),
            part, part, part, part, part, part,
            pltpu.SemaphoreType.DMA((3,)),
            pltpu.SemaphoreType.DMA((3, chunks)),
            pltpu.SemaphoreType.DMA((3, chunks)),
            pltpu.SemaphoreType.DMA((3, chunks)),
            pltpu.SemaphoreType.DMA((3, chunks)),
        ],
        compiler_params=pltpu.CompilerParams(
            collective_id=0, has_side_effects=True, vmem_limit_bytes=44 * 1024 * 1024
        ),
        cost_estimate=pl.CostEstimate(
            flops=pairs * HEAD_DIM * 4, bytes_accessed=4 * (2 * rows * width + 2 * keys * kv_width),
            transcendentals=pairs,
        ),
    )(valid_lengths, queries, visual_keys, projected_values)


def passed_along(shard, axis, by):
    size = lax.axis_size(axis)
    return lax.ppermute(shard, axis, [(i, (i + by) % size) for i in range(size)])


def attend(partial_value, query_tile, key_tile, value_tile, usable):
    peak_score, weight_sum, numerator = partial_value
    scores = jnp.einsum("qhgd,khd->hgqk", query_tile, key_tile, precision=lax.Precision.HIGHEST)
    scores = jnp.where(usable, scores, -1e30)
    new_peak = jnp.maximum(peak_score, jnp.max(scores, axis=-1))
    weights = jnp.where(usable, jnp.exp(scores - new_peak[..., None]), 0.0)
    factor = jnp.exp(peak_score - new_peak)
    weight_sum = weight_sum * factor + jnp.sum(weights, axis=-1)
    numerator = numerator * jnp.transpose(factor, (2, 0, 1))[..., None] + jnp.einsum(
        "hgqk,khd->qhgd", weights, value_tile, precision=lax.Precision.HIGHEST
    )
    return (new_peak, weight_sum, numerator)


def combine(upper_part, lower_part):
    new_peak = jnp.maximum(upper_part[0], lower_part[0])
    upper_factor = jnp.exp(upper_part[0] - new_peak)
    lower_factor = jnp.exp(lower_part[0] - new_peak)
    weight_sum = upper_part[1] * upper_factor + lower_part[1] * lower_factor
    numerator = (
        upper_part[2] * jnp.transpose(upper_factor, (2, 0, 1))[..., None]
        + lower_part[2] * jnp.transpose(lower_factor, (2, 0, 1))[..., None]
    )
    return (new_peak, weight_sum, numerator)


def per_device(queries, visual_keys, projected_values, valid_lengths):
    shard_blocks = lax.axis_size("blk")
    window = min(SPAN, shard_blocks // 2)
    left_reach = window // 2 - 1
    right_reach = window // 2
    device_pos = lax.axis_index("blk")
    query_rows = queries.shape[0]
    key_rows = visual_keys.shape[0]
    kv_heads = visual_keys.shape[1] // HEAD_DIM
    group_size = queries.shape[1] // (HEAD_DIM * kv_heads)
    query_tile = (queries * HEAD_DIM ** (-0.5)).reshape(query_rows, kv_heads, group_size, HEAD_DIM)
    key_tile = visual_keys.reshape(key_rows, kv_heads, HEAD_DIM)
    value_tile = projected_values.reshape(key_rows, kv_heads, HEAD_DIM)
    positions = jnp.arange(key_rows, dtype=jnp.int32)
    own_usable = positions < valid_lengths[0]
    initial = (
        jnp.full((kv_heads, group_size, query_rows), -1e30, jnp.float32),
        jnp.zeros((kv_heads, group_size, query_rows), jnp.float32),
        jnp.zeros((query_rows, kv_heads, group_size, HEAD_DIM), jnp.float32),
    )

    def query_usable(offset):
        owner_block = device_pos - offset
        return own_usable & (owner_block >= 0) & (owner_block < shard_blocks)

    upper_state = attend(initial, query_tile, key_tile, value_tile, query_usable(0))

    def climb_up(position, carried):
        arrived = passed_along((carried[0], carried[1], carried[2], carried[3]), "blk", 1)
        outcome = attend(
            (arrived[1], arrived[2], arrived[3]),
            arrived[0],
            key_tile,
            value_tile,
            query_usable(position),
        )
        return (arrived[0],) + outcome

    upper_carried = lax.fori_loop(1, right_reach + 1, climb_up, (query_tile,) + upper_state)
    upper_home = passed_along(
        (upper_carried[1], upper_carried[2], upper_carried[3]), "blk", -right_reach
    )
    lowering = passed_along(query_tile, "blk", -1)
    lower_state = attend(initial, lowering, key_tile, value_tile, query_usable(-1))

    def descend(position, carried):
        arrived = passed_along((carried[0], carried[1], carried[2], carried[3]), "blk", -1)
        outcome = attend(
            (arrived[1], arrived[2], arrived[3]),
            arrived[0],
            key_tile,
            value_tile,
            query_usable(-position),
        )
        return (arrived[0],) + outcome

    lower_carried = lax.fori_loop(2, left_reach + 1, descend, (lowering,) + lower_state)
    lower_home = passed_along(
        (lower_carried[1], lower_carried[2], lower_carried[3]), "blk", left_reach
    )
    final_state = combine(upper_home, lower_home)
    weight_sum = final_state[1]
    numerator = final_state[2]
    normed = numerator / jnp.transpose(weight_sum, (2, 0, 1))[..., None]
    return normed.reshape(query_rows, kv_heads * group_size * HEAD_DIM)


def solution(mesh):
    blocks = mesh.shape["blk"]
    body = paired if blocks % 2 == 0 and min(SPAN, blocks // 2) == 4 else per_device
    return jax.shard_map(
        body,
        mesh=mesh,
        in_specs=(P("blk", "heads"), P("blk", "heads"), P("blk", "heads"), P("blk")),
        out_specs=P("blk", "heads"),
        check_vma=False,
    )
```

```python
import functools
import math

import jax
import jax.numpy as jnp
from jax import lax
from jax.experimental import pallas as pl
from jax.experimental.pallas import tpu as pltpu
from jax.sharding import PartitionSpec as P

HEAD_DIM = 128
SPAN = 6
CH = 4
AHEAD = 2
EARLY = 2
SKEW = 2
MESH = pl.DeviceIdType.MESH
F32 = jnp.float32
BF16 = jnp.bfloat16


def split2(a):
    hi = a.astype(BF16)
    return hi, (a - hi.astype(F32)).astype(BF16)


def pair_kernel(
    blocks, group, n_ref, q_hbm, k_hbm, v_hbm, out_ref,
    kraw, vraw, ka, kb, va, q_own, qx, qz, qf,
    own_num, own_st, loc_num, loc_st,
    px_s, pz_s, pf_s, px_r, pz_r, pf_r,
    lsem, q_ss, q_rs, p_ss, p_rs,
):
    b = lax.axis_index("blk")
    x = lax.rem(b, 2)
    rows = q_own.shape[0]
    keys = kraw.shape[0]
    kv = kraw.shape[1] // HEAD_DIM
    chunks = q_own.shape[1] // (CH * HEAD_DIM)
    tb = rows // 8
    partner = b + 1 - 2 * x
    up, down = b + 2, b - 2
    has_up, has_down = up < blocks, down >= 0
    fdst, fsrc = b + 2 - 4 * x, b - 2 + 4 * x
    has_fdst = (fdst >= 0) & (fdst < blocks)
    has_fsrc = (fsrc >= 0) & (fsrc < blocks)

    barrier = pltpu.get_barrier_semaphore()
    pl.semaphore_signal(barrier, inc=1, device_id={"blk": partner}, device_id_type=MESH)

    @pl.when(has_up)
    def _():
        pl.semaphore_signal(barrier, inc=1, device_id={"blk": up}, device_id_type=MESH)

    @pl.when(has_down)
    def _():
        pl.semaphore_signal(barrier, inc=1, device_id={"blk": down}, device_id_type=MESH)

    own_copy = pltpu.make_async_copy(q_hbm, q_own, lsem.at[0])
    k_copy = pltpu.make_async_copy(k_hbm, kraw, lsem.at[1])
    v_copy = pltpu.make_async_copy(v_hbm, vraw, lsem.at[2])
    k_copy.start()
    v_copy.start()
    own_copy.start()
    pl.semaphore_wait(
        barrier, 1 + jnp.where(has_up, 1, 0) + jnp.where(has_down, 1, 0)
    )

    def cols(c):
        return pl.ds(pl.multiple_of(c * (CH * HEAD_DIM), CH * HEAD_DIM), CH * HEAD_DIM)

    def qcopy(kind, src, dst, c, to):
        return pltpu.make_async_remote_copy(
            src_ref=src.at[:, cols(c)], dst_ref=dst.at[:, cols(c)],
            send_sem=q_ss.at[kind, c], recv_sem=q_rs.at[kind, c],
            device_id={"blk": to}, device_id_type=MESH,
        )

    def x_copy(c):
        return qcopy(0, q_hbm, qx, c, partner)

    def z_copy(c):
        return qcopy(1, q_hbm, qz, c, up)

    def f_copy(c):
        return qcopy(2, qx, qf, c, fdst)

    def pcopy(kind, src, dst, c, to):
        return pltpu.make_async_remote_copy(
            src_ref=src.at[c], dst_ref=dst.at[c],
            send_sem=p_ss.at[kind, c], recv_sem=p_rs.at[kind, c],
            device_id={"blk": to}, device_id_type=MESH,
        )

    def px_copy(c):
        return pcopy(0, px_s, px_r, c, partner)

    def pz_copy(c):
        return pcopy(1, pz_s, pz_r, c, down)

    def pf_copy(c):
        return pcopy(2, pf_s, pf_r, c, fsrc)

    def start_x(c, carry):
        x_copy(c).start()
        return carry

    lax.fori_loop(0, min(AHEAD, chunks), start_x, 0)

    early = min(EARLY, chunks)

    def start_z(c, carry):
        z_copy(c).start()
        return carry

    @pl.when(has_up)
    def _():
        lax.fori_loop(0, early, start_z, 0)

    lane = lax.broadcasted_iota(jnp.int32, (rows, HEAD_DIM), 1)
    valid = n_ref[0]
    klane = lax.broadcasted_iota(jnp.int32, (keys, HEAD_DIM), 1)
    krow = lax.broadcasted_iota(jnp.int32, (keys, HEAD_DIM), 0)
    bias = jnp.where((klane == 0) & (krow >= valid), -1e30, 0.0).astype(BF16)
    k_copy.wait()
    for g in range(kv):
        hi, lo = split2(kraw[:, g * HEAD_DIM:(g + 1) * HEAD_DIM])
        ka[g, :, :HEAD_DIM] = hi
        ka[g, :, HEAD_DIM:] = hi
        kb[g, :, :HEAD_DIM] = lo
        kb[g, :, HEAD_DIM:] = bias
    v_copy.wait()
    for g in range(kv):
        hi, lo = split2(vraw[:, g * HEAD_DIM:(g + 1) * HEAD_DIM])
        va[g, :, :HEAD_DIM] = hi
        va[g, :, HEAD_DIM:] = lo
    own_copy.wait()

    qlane = lax.broadcasted_iota(jnp.int32, (CH * rows, HEAD_DIM), 1)
    one = jnp.where(qlane == 0, 1.0, 0.0).astype(BF16)
    scale = HEAD_DIM ** (-0.5) * math.log2(math.e)

    def attend(q_ref, c):
        g = (c * CH) // group
        q = q_ref[:, cols(c)]
        q = jnp.concatenate(
            [q[:, h * HEAD_DIM:(h + 1) * HEAD_DIM] for h in range(CH)], axis=0
        ) * scale
        hi, lo = split2(q)
        dims = (((1,), (1,)), ((), ()))
        s = lax.dot_general(
            jnp.concatenate([hi, lo], axis=1), ka[g], dims, preferred_element_type=F32
        ) + lax.dot_general(
            jnp.concatenate([hi, one], axis=1), kb[g], dims, preferred_element_type=F32
        )
        m = jnp.max(s, axis=1, keepdims=True)
        p = jnp.exp2(s - m)
        l = jnp.sum(p, axis=1, keepdims=True)
        p_hi, p_lo = split2(p)
        r = jnp.dot(p_hi, va[g], preferred_element_type=F32)
        num = r[:, :HEAD_DIM] + r[:, HEAD_DIM:] + jnp.dot(
            p_lo, va[g, :, :HEAD_DIM], preferred_element_type=F32
        )
        st = jnp.zeros((rows, HEAD_DIM), F32)
        for h in range(CH):
            st = jnp.where(lane == h, m[h * rows:(h + 1) * rows], st)
            st = jnp.where(lane == CH + h, l[h * rows:(h + 1) * rows], st)
        return num, st

    def pack(buf, c, num, st):
        buf[c, :CH * tb] = num.reshape(CH * tb, 8, HEAD_DIM)
        wide = jnp.concatenate([st] * (HEAD_DIM // rows), axis=0)
        buf[c, CH * tb] = wide.T[:8]

    def unpack(buf, c):
        num = buf[c, :CH * tb].reshape(CH * rows, HEAD_DIM)
        st = jnp.concatenate([buf[c, CH * tb]] * (HEAD_DIM // 8), axis=0).T[:rows]
        return num, st

    def column(st, h):
        return st[:, h:h + 1]

    def merge(a, o):
        top = jnp.maximum(a[1], o[1])
        fa, fo = jnp.exp2(a[1] - top), jnp.exp2(o[1] - top)
        total = a[1] * pltpu.roll(fa, CH, 1) + o[1] * pltpu.roll(fo, CH, 1)
        st = jnp.where(lane < CH, top, total)
        parts = []
        for h in range(CH):
            part = slice(h * rows, (h + 1) * rows)
            parts.append(a[0][part] * column(fa, h) + o[0][part] * column(fo, h))
        return jnp.concatenate(parts, axis=0), st

    def step(t, carry):
        zc = jnp.where(t < early, t, t - chunks)
        use_z = (t < early) | ((zc >= early) & (zc < chunks))
        fc = t - SKEW
        use_f = (fc >= 0) & (fc < chunks)
        mc = t - 2 * SKEW

        @pl.when(use_z)
        def _():
            num, st = attend(q_own, zc)
            own_num[zc] = num
            own_st[zc] = st

        @pl.when(use_f)
        def _():
            num, st = attend(qx, fc)
            loc_num[fc] = num
            loc_st[fc] = st

        @pl.when(t < chunks)
        def _():
            x_copy(t).wait_recv()

            @pl.when(has_fdst)
            def _():
                f_copy(t).start()

            x_copy(t).wait_send()

            @pl.when(t + AHEAD < chunks)
            def _():
                x_copy(t + AHEAD).start()

        @pl.when((t == chunks - 1) & has_up)
        def _():
            lax.fori_loop(early, chunks, start_z, 0)

        @pl.when(use_z & has_down)
        def _():
            z_copy(zc).wait_recv()
            num, st = attend(qz, zc)
            pack(pz_s, zc, num, st)
            pz_copy(zc).start()

        @pl.when(use_f & has_fsrc)
        def _():
            f_copy(fc).wait_recv()
            num, st = attend(qf, fc)
            pack(pf_s, fc, num, st)
            pf_copy(fc).start()

        @pl.when((mc >= 0) & (mc < chunks))
        def _():
            @pl.when(has_fdst)
            def _():
                pf_copy(mc).wait_recv()
                num, st = merge((loc_num[mc], loc_st[mc]), unpack(pf_r, mc))
                pack(px_s, mc, num, st)

            @pl.when(jnp.logical_not(has_fdst))
            def _():
                pack(px_s, mc, loc_num[mc], loc_st[mc])

            px_copy(mc).start()

        return carry

    lax.fori_loop(0, max(2 * chunks, chunks + 2 * SKEW), step, 0)

    def finish(c, carry):
        px_copy(c).wait_recv()
        num, st = merge((own_num[c], own_st[c]), unpack(px_r, c))
        own_num[c] = num
        own_st[c] = st

        @pl.when(has_up)
        def _():
            pz_copy(c).wait_recv()
            num, st = merge((own_num[c], own_st[c]), unpack(pz_r, c))
            own_num[c] = num
            own_st[c] = st

        st = own_st[c]
        num = own_num[c]
        out_ref[:, cols(c)] = jnp.concatenate(
            [num[h * rows:(h + 1) * rows] / column(st, CH + h) for h in range(CH)], axis=1
        )
        return carry

    lax.fori_loop(0, chunks, finish, 0)

    def drain(c, carry):
        px_copy(c).wait_send()

        @pl.when(has_up)
        def _():
            z_copy(c).wait_send()

        @pl.when(has_down)
        def _():
            pz_copy(c).wait_send()

        @pl.when(has_fdst)
        def _():
            f_copy(c).wait_send()

        @pl.when(has_fsrc)
        def _():
            pf_copy(c).wait_send()

        return carry

    lax.fori_loop(0, chunks, drain, 0)


def paired(queries, visual_keys, projected_values, valid_lengths):
    blocks = lax.axis_size("blk")
    rows, width = queries.shape
    keys, kv_width = visual_keys.shape
    kv = kv_width // HEAD_DIM
    group = width // kv_width
    chunks = width // (CH * HEAD_DIM)
    tiles = CH * rows // 8 + 1
    vmem = pltpu.VMEM
    part = vmem((chunks, tiles, 8, HEAD_DIM), F32)
    any_spec = pl.BlockSpec(memory_space=pl.ANY)
    pairs = 4 * rows * (width // HEAD_DIM) * keys
    return pl.pallas_call(
        functools.partial(pair_kernel, blocks, group),
        out_shape=jax.ShapeDtypeStruct((rows, width), F32),
        in_specs=[pl.BlockSpec(memory_space=pltpu.SMEM), any_spec, any_spec, any_spec],
        out_specs=pl.BlockSpec(memory_space=vmem),
        scratch_shapes=[
            vmem((keys, kv_width), F32),
            vmem((keys, kv_width), F32),
            vmem((kv, keys, 2 * HEAD_DIM), BF16),
            vmem((kv, keys, 2 * HEAD_DIM), BF16),
            vmem((kv, keys, 2 * HEAD_DIM), BF16),
            vmem((rows, width), F32),
            vmem((rows, width), F32),
            vmem((rows, width), F32),
            vmem((rows, width), F32),
            vmem((chunks, CH * rows, HEAD_DIM), F32),
            vmem((chunks, rows, HEAD_DIM), F32),
            vmem((chunks, CH * rows, HEAD_DIM), F32),
            vmem((chunks, rows, HEAD_DIM), F32),
            part, part, part, part, part, part,
            pltpu.SemaphoreType.DMA((3,)),
            pltpu.SemaphoreType.DMA((3, chunks)),
            pltpu.SemaphoreType.DMA((3, chunks)),
            pltpu.SemaphoreType.DMA((3, chunks)),
            pltpu.SemaphoreType.DMA((3, chunks)),
        ],
        compiler_params=pltpu.CompilerParams(
            collective_id=0, has_side_effects=True, vmem_limit_bytes=62 * 1024 * 1024
        ),
        cost_estimate=pl.CostEstimate(
            flops=pairs * HEAD_DIM * 4, bytes_accessed=4 * (2 * rows * width + 2 * keys * kv_width),
            transcendentals=pairs,
        ),
    )(valid_lengths, queries, visual_keys, projected_values)


def passed_along(shard, axis, by):
    size = lax.axis_size(axis)
    return lax.ppermute(shard, axis, [(i, (i + by) % size) for i in range(size)])


def attend(partial_value, query_tile, key_tile, value_tile, usable):
    peak_score, weight_sum, numerator = partial_value
    scores = jnp.einsum("qhgd,khd->hgqk", query_tile, key_tile, precision=lax.Precision.HIGHEST)
    scores = jnp.where(usable, scores, -1e30)
    new_peak = jnp.maximum(peak_score, jnp.max(scores, axis=-1))
    weights = jnp.where(usable, jnp.exp(scores - new_peak[..., None]), 0.0)
    factor = jnp.exp(peak_score - new_peak)
    weight_sum = weight_sum * factor + jnp.sum(weights, axis=-1)
    numerator = numerator * jnp.transpose(factor, (2, 0, 1))[..., None] + jnp.einsum(
        "hgqk,khd->qhgd", weights, value_tile, precision=lax.Precision.HIGHEST
    )
    return (new_peak, weight_sum, numerator)


def combine(upper_part, lower_part):
    new_peak = jnp.maximum(upper_part[0], lower_part[0])
    upper_factor = jnp.exp(upper_part[0] - new_peak)
    lower_factor = jnp.exp(lower_part[0] - new_peak)
    weight_sum = upper_part[1] * upper_factor + lower_part[1] * lower_factor
    numerator = (
        upper_part[2] * jnp.transpose(upper_factor, (2, 0, 1))[..., None]
        + lower_part[2] * jnp.transpose(lower_factor, (2, 0, 1))[..., None]
    )
    return (new_peak, weight_sum, numerator)


def per_device(queries, visual_keys, projected_values, valid_lengths):
    shard_blocks = lax.axis_size("blk")
    window = min(SPAN, shard_blocks // 2)
    left_reach = window // 2 - 1
    right_reach = window // 2
    device_pos = lax.axis_index("blk")
    query_rows = queries.shape[0]
    key_rows = visual_keys.shape[0]
    kv_heads = visual_keys.shape[1] // HEAD_DIM
    group_size = queries.shape[1] // (HEAD_DIM * kv_heads)
    query_tile = (queries * HEAD_DIM ** (-0.5)).reshape(query_rows, kv_heads, group_size, HEAD_DIM)
    key_tile = visual_keys.reshape(key_rows, kv_heads, HEAD_DIM)
    value_tile = projected_values.reshape(key_rows, kv_heads, HEAD_DIM)
    positions = jnp.arange(key_rows, dtype=jnp.int32)
    own_usable = positions < valid_lengths[0]
    initial = (
        jnp.full((kv_heads, group_size, query_rows), -1e30, jnp.float32),
        jnp.zeros((kv_heads, group_size, query_rows), jnp.float32),
        jnp.zeros((query_rows, kv_heads, group_size, HEAD_DIM), jnp.float32),
    )

    def query_usable(offset):
        owner_block = device_pos - offset
        return own_usable & (owner_block >= 0) & (owner_block < shard_blocks)

    upper_state = attend(initial, query_tile, key_tile, value_tile, query_usable(0))

    def climb_up(position, carried):
        arrived = passed_along((carried[0], carried[1], carried[2], carried[3]), "blk", 1)
        outcome = attend(
            (arrived[1], arrived[2], arrived[3]),
            arrived[0],
            key_tile,
            value_tile,
            query_usable(position),
        )
        return (arrived[0],) + outcome

    upper_carried = lax.fori_loop(1, right_reach + 1, climb_up, (query_tile,) + upper_state)
    upper_home = passed_along(
        (upper_carried[1], upper_carried[2], upper_carried[3]), "blk", -right_reach
    )
    lowering = passed_along(query_tile, "blk", -1)
    lower_state = attend(initial, lowering, key_tile, value_tile, query_usable(-1))

    def descend(position, carried):
        arrived = passed_along((carried[0], carried[1], carried[2], carried[3]), "blk", -1)
        outcome = attend(
            (arrived[1], arrived[2], arrived[3]),
            arrived[0],
            key_tile,
            value_tile,
            query_usable(-position),
        )
        return (arrived[0],) + outcome

    lower_carried = lax.fori_loop(2, left_reach + 1, descend, (lowering,) + lower_state)
    lower_home = passed_along(
        (lower_carried[1], lower_carried[2], lower_carried[3]), "blk", left_reach
    )
    final_state = combine(upper_home, lower_home)
    weight_sum = final_state[1]
    numerator = final_state[2]
    normed = numerator / jnp.transpose(weight_sum, (2, 0, 1))[..., None]
    return normed.reshape(query_rows, kv_heads * group_size * HEAD_DIM)


def solution(mesh):
    blocks = mesh.shape["blk"]
    body = paired if blocks % 2 == 0 and min(SPAN, blocks // 2) == 4 else per_device
    return jax.shard_map(
        body,
        mesh=mesh,
        in_specs=(P("blk", "heads"), P("blk", "heads"), P("blk", "heads"), P("blk")),
        out_specs=P("blk", "heads"),
        check_vma=False,
    )
```
